32 devices in a mesh: ray: 4 (over y, x), cell: 8 (over z, core).
Axes of the slice: x: 2, y: 2, z: 4, core: 2. Of those that a mesh axis runs over, the one named last changes fastest.
Arguments:
- probes: bfloat16 [4096, 128], P('cell'), may hold values from -6 to 6
- prior: float32 [4096], P('cell'), may hold values from 0.5 to 2
- tiles: bfloat16 [4, 8, 720, 128, 128], P('ray', 'cell'), may hold values from -0.078125 to 0.078125
- tile_ray: int32 [4, 8, 720], P('ray', 'cell'), may hold values from 0 to 15
- tile_cell: int32 [4, 8, 720], P('ray', 'cell'), may hold values from 0 to 31, as said below
- tile_count: int32 [4, 8], P('ray', 'cell'), may hold values from 360 to 720, as said below
- noise: float32 [4, 8, 2048], P('ray', 'cell'), may hold values from 0.25 to 4
Outputs:
- basis: float32 [4096, 128], P('cell')
- factor: float32 [128, 128], replicated
The draws below stay inside these ranges and needn't reach their ends.
Inputs may be any that keep to these rules, and one draw needn't show every extreme that they name: `tile_count`: every device has between half of 720 and 720 live tile slots; in every draw some device has all 720 live. `tile_cell`: the slots of device (r, c) name only cell blocks of the owners c - 3 to c + 3 that exist, that is blocks max(c - 3, 0) * 4 up to (c + 4) * 4 - 1 or the last block.
All inputs are finite; a program needn't handle non-finite values.
Results may differ from the reference program's by a relative error of at most 0.0031.
Values may be sent and summed in bfloat16 or wider, within the bound.
A program may use at most 256 MiB of HBM per device.

```python
import math
import jax
import jax.numpy as jnp
from jax import lax

TB = 128
K = 128
REACH = 3
CBD = 4
RBD = 16
TPR = 45
TILES = 720
NCB = 32
CELLS = 4096
N_RAY = 4
N_CELL = 8


def draw_tile_count(key, part):
    count_key, full_key = jax.random.split(jax.random.fold_in(key, 11))
    device_total = N_RAY * N_CELL
    counts = jax.random.randint(count_key, (device_total,), TILES // 2, TILES + 1, dtype=jnp.int32)
    full_at = jax.random.randint(full_key, (), 0, device_total, dtype=jnp.int32)
    counts = jnp.where(jnp.arange(device_total, dtype=jnp.int32) == full_at, TILES, counts)
    return counts.reshape(N_RAY, N_CELL)


def draw_tile_cell(key, part):
    owner_index = jnp.arange(N_CELL, dtype=jnp.int32)
    window_low = jnp.maximum(owner_index - REACH, 0) * CBD
    window_high = jnp.minimum(owner_index + REACH + 1, N_CELL) * CBD
    low_all = jnp.broadcast_to(window_low[None, :, None], (N_RAY, N_CELL, TILES))
    high_all = jnp.broadcast_to(window_high[None, :, None], (N_RAY, N_CELL, TILES))
    return jax.random.randint(jax.random.fold_in(key, 23), (N_RAY, N_CELL, TILES), low_all, high_all, dtype=jnp.int32)


def set_ends(values, key, low, top_value):
    longest = values.shape.index(max(values.shape))
    spots = []
    for shift in (0, 1):
        where = [jax.random.randint(jax.random.fold_in(key, axis), (), 0, length) for axis, length in enumerate(values.shape)]
        where[longest] = (where[longest] + shift) % values.shape[longest]
        spots.append(tuple(where))
    return values.at[spots[0]].set(low).at[spots[1]].set(top_value)


def block_levels(rng, shape, pieces, low, top_value):
    def one(axis_at, blocks):
        heights = jax.random.uniform(jax.random.fold_in(jax.random.fold_in(rng, 6), axis_at), (blocks,), jnp.float32, low / len(pieces), top_value / len(pieces))
        return jnp.repeat(jnp.exp(heights), shape[axis_at] // blocks).reshape((-1,) + (1,) * (len(shape) - axis_at - 1))

    factor_of = one(*pieces[0])
    for cut in pieces[1:]:
        factor_of = factor_of * one(*cut)
    return factor_of


def bell_draw(stream_key, shape, deviation, bound, shards=(), kind=jnp.bfloat16):
    array = jax.random.normal(stream_key, shape, jnp.float32) * deviation
    if len(shards) > 0:
        array = block_levels(stream_key, shape, shards, -0.22, 0.18) * array
    return jnp.clip(array, min=-bound, max=bound).astype(kind)


def setup_inputs(seed: int = 0) -> dict:
    streams_of = jax.random.split(jax.random.key(seed), 8)
    probes = bell_draw(streams_of[0], (CELLS, K), 1.0, 6.0, ((0, 8),))
    prior = jnp.clip(jnp.exp(math.log(2.0) - 1.3862944 * jax.random.uniform(streams_of[1], (CELLS,), jnp.float32) ** block_levels(streams_of[1], (CELLS,), ((0, 8),), -0.2, 0.2)), 0.5, 2.0)
    tiles = bell_draw(streams_of[2], (N_RAY, N_CELL, TILES, TB, TB), (TPR * TB) ** -0.5, 0.078125, ((0, 4), (1, 8)))
    tile_ray = set_ends(jax.random.randint(streams_of[3], (N_RAY, N_CELL, TILES), 0, RBD), jax.random.fold_in(streams_of[3], 1), 0, RBD - 1).astype(jnp.int32)
    tile_cell = draw_tile_cell(jax.random.fold_in(streams_of[7], 71), 0)
    tile_count = draw_tile_count(jax.random.fold_in(streams_of[7], 71), 0)
    noise = jnp.clip(jnp.exp(math.log(4.0) - 2.7725887 * jax.random.uniform(streams_of[6], (N_RAY, N_CELL, RBD * TB), jnp.float32) ** block_levels(streams_of[6], (N_RAY, N_CELL, RBD * TB), ((0, 4), (1, 8)), -0.2, 0.2)), 0.25, 4.0)
    return dict(probes=probes, prior=prior, tiles=tiles, tile_ray=tile_ray, tile_cell=tile_cell, tile_count=tile_count, noise=noise)


def orthonormal(rows_all):
    gram_matrix = jnp.dot(rows_all.T, rows_all, precision=lax.Precision.HIGHEST)
    lower_factor = jnp.linalg.cholesky(gram_matrix)
    result = jax.scipy.linalg.solve_triangular(lower_factor, rows_all.T, lower=True).T
    return (result, lower_factor)

def device_partial(tile_set, ray_index, columns, live_count, weights, blocks):
    slot_total = tile_set.shape[0]
    live_slot = jnp.arange(slot_total, dtype=jnp.int32) < live_count
    padded = jnp.concatenate([blocks, jnp.zeros((1, TB, K), jnp.bfloat16)], axis=0)
    picked = padded[jnp.where(live_slot, columns, NCB).astype(jnp.int32)]
    product = jnp.einsum('tij,tjk->tik', tile_set.astype(jnp.float32), picked.astype(jnp.float32))
    forward = jax.ops.segment_sum(product, ray_index, num_segments=RBD)
    weighted = (weights.reshape(RBD, TB, 1) * forward).astype(jnp.bfloat16)
    wpadded = jnp.concatenate([weighted, jnp.zeros((1, TB, K), jnp.bfloat16)], axis=0)
    back_rows = wpadded[jnp.where(live_slot, ray_index, RBD).astype(jnp.int32)]
    backward = jnp.einsum('tij,tik->tjk', tile_set.astype(jnp.float32), back_rows.astype(jnp.float32))
    return jax.ops.segment_sum(backward, columns, num_segments=NCB).reshape(CELLS, K)

def reference(probes, prior, tiles, tile_ray, tile_cell, tile_count, noise):
    scaled = (prior[:, None] * probes.astype(jnp.float32)).astype(jnp.bfloat16)
    blocks = scaled.reshape(NCB, TB, K)
    devices_all = N_RAY * N_CELL
    inputs = (tiles.reshape(devices_all, TILES, TB, TB), tile_ray.reshape(devices_all, TILES), tile_cell.reshape(devices_all, TILES), tile_count.reshape(devices_all), noise.reshape(devices_all, RBD * TB))

    def accumulate(running, device_item):
        return (running + device_partial(device_item[0], device_item[1], device_item[2], device_item[3], device_item[4], blocks), None)
    gradient, _ = lax.scan(accumulate, jnp.zeros((CELLS, K), jnp.float32), inputs)
    sample = prior[:, None] * gradient
    basis_raw, lower_factor = orthonormal(sample)
    root_cells = jnp.sqrt(jnp.float32(CELLS))
    return (basis_raw * root_cells, lower_factor.T / root_cells)
```

```python
import functools
import jax
import jax.numpy as jnp
from jax import lax
from jax.experimental import pallas as pl
from jax.experimental.pallas import tpu as pltpu
from jax.sharding import PartitionSpec as P

REACH = 3


def k2_kernel(group, chunk, ray_ref, cell_ref, count_ref, win_ref, noise_ref, tiles_hbm, out_ref, tiles, fwd, wt, bwd, sems):
    slots, edge = tiles.shape[0], tiles.shape[1]
    nb = noise_ref.shape[0]
    wb = win_ref.shape[0]
    chunks = slots // chunk
    def cp(i):
        s = pl.ds(pl.multiple_of(i * chunk, chunk), chunk)
        return pltpu.make_async_copy(tiles_hbm.at[s], tiles.at[s], sems.at[i])
    @pl.loop(0, chunks)
    def _(i):
        cp(i).start()
    fwd[...] = jnp.zeros_like(fwd)
    bwd[...] = jnp.zeros_like(bwd)
    count = count_ref[0]
    @pl.loop(0, chunks)
    def _(i):
        cp(i).wait()
        @pl.loop(0, chunk // group)
        def _(j):
            t0 = i * chunk + j * group
            prods = []
            for g in range(group):
                t = t0 + g
                prods.append(jnp.dot(tiles[t], win_ref[cell_ref[t]], preferred_element_type=jnp.float32))
            for g in range(group):
                t = t0 + g
                b = jnp.where(t < count, ray_ref[t], nb)
                fwd[b] = fwd[b] + prods[g]
    @pl.loop(0, nb)
    def _(b):
        wt[b] = (fwd[b].T * noise_ref[pl.ds(b, 1), :]).astype(jnp.bfloat16)
    @pl.loop(0, slots // group)
    def _(j):
        t0 = j * group
        prods = []
        for g in range(group):
            t = t0 + g
            prods.append(jnp.dot(wt[ray_ref[t]], tiles[t], preferred_element_type=jnp.float32))
        for g in range(group):
            t = t0 + g
            q = jnp.where(t < count, cell_ref[t], wb)
            bwd[q] = bwd[q] + prods[g]
    @pl.loop(0, wb)
    def _(q):
        out_ref[q] = bwd[q].astype(jnp.bfloat16)

def k2(win, tiles, ray, cell, count, noise, group=48, chunk=48):
    S, E = tiles.shape[0], tiles.shape[1]
    nb, wb = noise.shape[0], win.shape[0]
    V = pl.BlockSpec(memory_space=pltpu.VMEM); M = pl.BlockSpec(memory_space=pltpu.SMEM)
    return pl.pallas_call(functools.partial(k2_kernel, group, chunk),
        out_shape=jax.ShapeDtypeStruct((wb, 128, E), jnp.bfloat16),
        in_specs=[M, M, M, V, V, pl.BlockSpec(memory_space=pl.ANY)], out_specs=V,
        scratch_shapes=[pltpu.VMEM(tiles.shape, jnp.bfloat16), pltpu.VMEM((nb+1, E, 128), jnp.float32),
            pltpu.VMEM((nb, 128, E), jnp.bfloat16), pltpu.VMEM((wb+1, 128, E), jnp.float32), pltpu.SemaphoreType.DMA((S//chunk,))],
        compiler_params=pltpu.CompilerParams(vmem_limit_bytes=48*2**20),
        )(ray, cell, count, win, noise, tiles)


def passed_along(value, axis, by):
    length = lax.axis_size(axis)
    pairs = [(i, i + by) for i in range(length) if 0 <= i + by < length]
    return lax.ppermute(value, axis, pairs)


def summed(value, axis):
    length = lax.axis_size(axis)
    step = 1
    while step < length:
        value = value + lax.ppermute(value, axis, [(i, i ^ step) for i in range(length)])
        step *= 2
    return value


def local(probes, prior, tiles, tile_ray, tile_cell, tile_count, noise):
    edge = tiles.shape[-1]
    width = probes.shape[1]
    own_rows = probes.shape[0]
    own_blocks = own_rows // edge
    owner_total = lax.axis_size("cell")
    owner_index = lax.axis_index("cell")
    span = 2 * REACH + 1
    scaled = (prior[:, None] * probes.astype(jnp.float32)).astype(jnp.bfloat16)
    window = jnp.concatenate(
        [scaled if d == 0 else passed_along(scaled, "cell", -d) for d in range(-REACH, REACH + 1)],
        axis=0,
    ).reshape(span * own_blocks, edge, width)
    local_block = tile_cell[0, 0] - (owner_index - REACH) * own_blocks
    partial = k2(
        window,
        tiles[0, 0],
        tile_ray[0, 0],
        local_block,
        tile_count[0],
        noise[0, 0].reshape(-1, edge),
    ).reshape(span, own_blocks, width, edge)
    own = partial[REACH].astype(jnp.float32)
    for d in range(-REACH, REACH + 1):
        if d != 0:
            own = own + passed_along(partial[REACH + d], "cell", d).astype(jnp.float32)
    root_cells = jnp.sqrt(jnp.float32(own_rows * owner_total))
    gradient = summed(own, "ray")
    sample = prior.reshape(own_blocks, 1, edge) * gradient
    sample = sample.transpose(1, 0, 2).reshape(width, own_rows)
    gram = summed(jnp.dot(sample, sample.T, precision=lax.Precision.HIGHEST), "cell")
    lower = jnp.linalg.cholesky(gram)
    basis = jax.scipy.linalg.solve_triangular(lower, sample, lower=True).T
    return (basis * root_cells, lower.T / root_cells)


def solution(mesh):
    placed = (
        P("cell", None),
        P("cell"),
        P("ray", "cell", None, None, None),
        P("ray", "cell", None),
        P("ray", "cell", None),
        P("ray", "cell"),
        P("ray", "cell", None),
    )
    return jax.shard_map(
        local, mesh=mesh, in_specs=placed, out_specs=(P("cell", None), P()), check_vma=False
    )
```

```python
import functools
import jax
import jax.numpy as jnp
from jax import lax
from jax.experimental import pallas as pl
from jax.experimental.pallas import tpu as pltpu
from jax.sharding import PartitionSpec as P

REACH = 3


def k2_kernel(group, chunk, ray_ref, cell_ref, count_ref, win_ref, noise_ref, tiles_hbm, out_ref, tiles, fwd, wt, bwd, sems):
    slots, edge = tiles.shape[0], tiles.shape[1]
    nb = noise_ref.shape[0]
    wb = win_ref.shape[0]
    chunks = slots // chunk
    def cp(i):
        s = pl.ds(pl.multiple_of(i * chunk, chunk), chunk)
        return pltpu.make_async_copy(tiles_hbm.at[s], tiles.at[s], sems.at[i])
    @pl.loop(0, chunks)
    def _(i):
        cp(i).start()
    fwd[...] = jnp.zeros_like(fwd)
    bwd[...] = jnp.zeros_like(bwd)
    count = count_ref[0]
    @pl.loop(0, chunks)
    def _(i):
        cp(i).wait()
        @pl.loop(0, chunk // group)
        def _(j):
            t0 = i * chunk + j * group
            prods = []
            for g in range(group):
                t = t0 + g
                prods.append(jnp.dot(tiles[t], win_ref[cell_ref[t]], preferred_element_type=jnp.float32))
            for g in range(group):
                t = t0 + g
                b = jnp.where(t < count, ray_ref[t], nb)
                fwd[b] = fwd[b] + prods[g]
    @pl.loop(0, nb)
    def _(b):
        wt[b] = (fwd[b].T * noise_ref[pl.ds(b, 1), :]).astype(jnp.bfloat16)
    @pl.loop(0, slots // group)
    def _(j):
        t0 = j * group
        prods = []
        for g in range(group):
            t = t0 + g
            prods.append(jnp.dot(wt[ray_ref[t]], tiles[t], preferred_element_type=jnp.float32))
        for g in range(group):
            t = t0 + g
            q = jnp.where(t < count, cell_ref[t], wb)
            bwd[q] = bwd[q] + prods[g]
    @pl.loop(0, wb)
    def _(q):
        out_ref[q] = bwd[q].astype(jnp.bfloat16)

def k2(win, tiles, ray, cell, count, noise, group=72, chunk=72):
    S, E = tiles.shape[0], tiles.shape[1]
    nb, wb = noise.shape[0], win.shape[0]
    V = pl.BlockSpec(memory_space=pltpu.VMEM); M = pl.BlockSpec(memory_space=pltpu.SMEM)
    return pl.pallas_call(functools.partial(k2_kernel, group, chunk),
        out_shape=jax.ShapeDtypeStruct((wb, 128, E), jnp.bfloat16),
        in_specs=[M, M, M, V, V, pl.BlockSpec(memory_space=pl.ANY)], out_specs=V,
        scratch_shapes=[pltpu.VMEM(tiles.shape, jnp.bfloat16), pltpu.VMEM((nb+1, E, 128), jnp.float32),
            pltpu.VMEM((nb, 128, E), jnp.bfloat16), pltpu.VMEM((wb+1, 128, E), jnp.float32), pltpu.SemaphoreType.DMA((S//chunk,))],
        compiler_params=pltpu.CompilerParams(vmem_limit_bytes=48*2**20),
        )(ray, cell, count, win, noise, tiles)


def passed_along(value, axis, by):
    length = lax.axis_size(axis)
    pairs = [(i, i + by) for i in range(length) if 0 <= i + by < length]
    return lax.ppermute(value, axis, pairs)


def summed(value, axis, kind=jnp.float32):
    length = lax.axis_size(axis)
    step = 1
    while step < length:
        sent = value.astype(kind)
        got = lax.ppermute(sent, axis, [(i, i ^ step) for i in range(length)])
        value = sent.astype(jnp.float32) + got.astype(jnp.float32)
        step *= 2
    return value


def local(probes, prior, tiles, tile_ray, tile_cell, tile_count, noise):
    edge = tiles.shape[-1]
    width = probes.shape[1]
    own_rows = probes.shape[0]
    own_blocks = own_rows // edge
    owner_total = lax.axis_size("cell")
    owner_index = lax.axis_index("cell")
    span = 2 * REACH + 1
    scaled = (prior[:, None] * probes.astype(jnp.float32)).astype(jnp.bfloat16)
    window = jnp.concatenate(
        [scaled if d == 0 else passed_along(scaled, "cell", -d) for d in range(-REACH, REACH + 1)],
        axis=0,
    ).reshape(span * own_blocks, edge, width)
    local_block = tile_cell[0, 0] - (owner_index - REACH) * own_blocks
    partial = k2(
        window,
        tiles[0, 0],
        tile_ray[0, 0],
        local_block,
        tile_count[0],
        noise[0, 0].reshape(-1, edge),
    ).reshape(span, own_blocks, width, edge)
    own = partial[REACH].astype(jnp.float32)
    for d in range(-REACH, REACH + 1):
        if d != 0:
            own = own + passed_along(partial[REACH + d], "cell", d).astype(jnp.float32)
    root_cells = jnp.sqrt(jnp.float32(own_rows * owner_total))
    gradient = summed(own, "ray", jnp.bfloat16)
    sample = prior.reshape(own_blocks, 1, edge) * gradient
    sample = sample.transpose(1, 0, 2).reshape(width, own_rows)
    gram = summed(jnp.dot(sample, sample.T, precision=lax.Precision.HIGHEST), "cell")
    lower = jnp.linalg.cholesky(gram)
    basis = jax.scipy.linalg.solve_triangular(lower, sample, lower=True).T
    return (basis * root_cells, lower.T / root_cells)


def solution(mesh):
    placed = (
        P("cell", None),
        P("cell"),
        P("ray", "cell", None, None, None),
        P("ray", "cell", None),
        P("ray", "cell", None),
        P("ray", "cell"),
        P("ray", "cell", None),
    )
    return jax.shard_map(
        local, mesh=mesh, in_specs=placed, out_specs=(P("cell", None), P()), check_vma=False
    )
```

```python
import functools
import jax
import jax.numpy as jnp
from jax import lax
from jax.experimental import pallas as pl
from jax.experimental.pallas import tpu as pltpu
from jax.sharding import PartitionSpec as P

REACH = 3


def k2_kernel(group, chunk, ray_ref, cell_ref, count_ref, win_ref, noise_ref, tiles_hbm, out_ref, tiles, fwd, wt, bwd, sems):
    slots, edge = tiles.shape[0], tiles.shape[1]
    nb = noise_ref.shape[0]
    wb = win_ref.shape[0]
    chunks = slots // chunk
    def cp(i):
        s = pl.ds(pl.multiple_of(i * chunk, chunk), chunk)
        return pltpu.make_async_copy(tiles_hbm.at[s], tiles.at[s], sems.at[i])
    @pl.loop(0, chunks)
    def _(i):
        cp(i).start()
    fwd[...] = jnp.zeros_like(fwd)
    bwd[...] = jnp.zeros_like(bwd)
    count = count_ref[0]
    @pl.loop(0, chunks)
    def _(i):
        cp(i).wait()
        @pl.loop(0, chunk // group)
        def _(j):
            t0 = i * chunk + j * group
            prods = []
            for g in range(group):
                t = t0 + g
                prods.append(jnp.dot(tiles[t], win_ref[cell_ref[t]], preferred_element_type=jnp.float32))
            for g in range(group):
                t = t0 + g
                b = jnp.where(t < count, ray_ref[t], nb)
                fwd[b] = fwd[b] + prods[g]
    @pl.loop(0, nb)
    def _(b):
        wt[b] = (fwd[b].T * noise_ref[pl.ds(b, 1), :]).astype(jnp.bfloat16)
    @pl.loop(0, slots // group)
    def _(j):
        t0 = j * group
        prods = []
        for g in range(group):
            t = t0 + g
            prods.append(jnp.dot(wt[ray_ref[t]], tiles[t], preferred_element_type=jnp.float32))
        for g in range(group):
            t = t0 + g
            q = jnp.where(t < count, cell_ref[t], wb)
            bwd[q] = bwd[q] + prods[g]
    @pl.loop(0, wb)
    def _(q):
        out_ref[q] = bwd[q].astype(jnp.bfloat16)

def k2(win, tiles, ray, cell, count, noise, group=72, chunk=72):
    S, E = tiles.shape[0], tiles.shape[1]
    nb, wb = noise.shape[0], win.shape[0]
    V = pl.BlockSpec(memory_space=pltpu.VMEM); M = pl.BlockSpec(memory_space=pltpu.SMEM)
    return pl.pallas_call(functools.partial(k2_kernel, group, chunk),
        out_shape=jax.ShapeDtypeStruct((wb, 128, E), jnp.bfloat16),
        in_specs=[M, M, M, V, V, pl.BlockSpec(memory_space=pl.ANY)], out_specs=V,
        scratch_shapes=[pltpu.VMEM(tiles.shape, jnp.bfloat16), pltpu.VMEM((nb+1, E, 128), jnp.float32),
            pltpu.VMEM((nb, 128, E), jnp.bfloat16), pltpu.VMEM((wb+1, 128, E), jnp.float32), pltpu.SemaphoreType.DMA((S//chunk,))],
        compiler_params=pltpu.CompilerParams(vmem_limit_bytes=48*2**20),
        )(ray, cell, count, win, noise, tiles)


def finish_kernel(root, gram_ref, sample_ref, basis_ref, factor_ref, work):
    n = gram_ref.shape[0]
    row_at = lax.broadcasted_iota(jnp.int32, (n, n), 0)
    col_at = lax.broadcasted_iota(jnp.int32, (n, n), 1)
    work[:, :n] = gram_ref[...]
    work[:, n:] = jnp.where(row_at == col_at, 1.0, 0.0)
    inside = lax.broadcasted_iota(jnp.int32, (8, n), 0)
    for first in range(0, n, 8):
        panel = work[first : first + 8, :]
        cols = [
            jnp.broadcast_to(panel[:, first + i : first + i + 1], (8, n)) for i in range(8)
        ]
        halves = [panel[:, :n], panel[:, n:]]
        for i in range(8):
            scale = lax.rsqrt(jnp.broadcast_to(cols[i][i : i + 1, :], (8, n)))
            coef = jnp.where(inside > i, cols[i] * scale, 0.0)
            for j in range(i + 1, 8):
                cols[j] = cols[j] - coef * (cols[j][i : i + 1, :] * scale)
            for h in range(2):
                pivot = halves[h][i : i + 1, :] * scale
                halves[h] = jnp.where(inside == i, pivot, halves[h] - coef * pivot)
        panel = jnp.concatenate(halves, axis=1)
        work[first : first + 8, :] = panel
        if first + 8 < n:
            update = lax.dot_general(
                panel[:, :n],
                panel,
                (((0,), (0,)), ((), ())),
                precision=lax.Precision.HIGHEST,
                preferred_element_type=jnp.float32,
            )
            work[first + 8 :, :] = work[first + 8 :, :] - update[first + 8 :, :]
    factor_ref[...] = jnp.where(row_at <= col_at, work[:, :n], 0.0) / root
    inverse = jnp.where(row_at >= col_at, work[:, n:], 0.0)
    rows = jnp.dot(
        inverse, sample_ref[...], precision=lax.Precision.HIGHEST, preferred_element_type=jnp.float32
    )
    basis_ref[...] = rows.T * root


def finish(gram, sample, root):
    n, rows = sample.shape
    return pl.pallas_call(
        functools.partial(finish_kernel, root),
        out_shape=(
            jax.ShapeDtypeStruct((rows, n), jnp.float32),
            jax.ShapeDtypeStruct((n, n), jnp.float32),
        ),
        in_specs=[pl.BlockSpec(memory_space=pltpu.VMEM)] * 2,
        out_specs=(pl.BlockSpec(memory_space=pltpu.VMEM),) * 2,
        scratch_shapes=[pltpu.VMEM((n, 2 * n), jnp.float32)],
        compiler_params=pltpu.CompilerParams(vmem_limit_bytes=16 * 2**20),
    )(gram, sample)


def passed_along(value, axis, by):
    length = lax.axis_size(axis)
    pairs = [(i, i + by) for i in range(length) if 0 <= i + by < length]
    return lax.ppermute(value, axis, pairs)


def summed(value, axis, kind=jnp.float32):
    length = lax.axis_size(axis)
    step = 1
    while step < length:
        sent = value.astype(kind)
        got = lax.ppermute(sent, axis, [(i, i ^ step) for i in range(length)])
        value = sent.astype(jnp.float32) + got.astype(jnp.float32)
        step *= 2
    return value


def local(probes, prior, tiles, tile_ray, tile_cell, tile_count, noise):
    edge = tiles.shape[-1]
    width = probes.shape[1]
    own_rows = probes.shape[0]
    own_blocks = own_rows // edge
    owner_total = lax.axis_size("cell")
    owner_index = lax.axis_index("cell")
    span = 2 * REACH + 1
    scaled = (prior[:, None] * probes.astype(jnp.float32)).astype(jnp.bfloat16)
    window = jnp.concatenate(
        [scaled if d == 0 else passed_along(scaled, "cell", -d) for d in range(-REACH, REACH + 1)],
        axis=0,
    ).reshape(span * own_blocks, edge, width)
    local_block = tile_cell[0, 0] - (owner_index - REACH) * own_blocks
    partial = k2(
        window,
        tiles[0, 0],
        tile_ray[0, 0],
        local_block,
        tile_count[0],
        noise[0, 0].reshape(-1, edge),
    ).reshape(span, own_blocks, width, edge)
    own = partial[REACH].astype(jnp.float32)
    for d in range(-REACH, REACH + 1):
        if d != 0:
            own = own + passed_along(partial[REACH + d], "cell", d).astype(jnp.float32)
    root_cells = float(own_rows * owner_total) ** 0.5
    gradient = summed(own, "ray", jnp.bfloat16)
    sample = prior.reshape(own_blocks, 1, edge) * gradient
    sample = sample.transpose(1, 0, 2).reshape(width, own_rows)
    gram = summed(jnp.dot(sample, sample.T, precision=lax.Precision.HIGHEST), "cell")
    return finish(gram, sample, root_cells)


def solution(mesh):
    placed = (
        P("cell", None),
        P("cell"),
        P("ray", "cell", None, None, None),
        P("ray", "cell", None),
        P("ray", "cell", None),
        P("ray", "cell"),
        P("ray", "cell", None),
    )
    return jax.shard_map(
        local, mesh=mesh, in_specs=placed, out_specs=(P("cell", None), P()), check_vma=False
    )
```
